32 devices in a mesh: groups: 1, fsdp: 32 (over z, y, x, core).
Axes of the slice: x: 2, y: 2, z: 4, core: 2. Of those that a mesh axis runs over, the one named last changes fastest.
Arguments:
- tokens: bfloat16 [8192, 8192], P(('groups', 'fsdp')), may hold values from -6 to 6
- frozen_value_weight: bfloat16 [8192, 1024], P('fsdp'), may hold values from -0.0625 to 0.0625
- adapter_down_weight: bfloat16 [8192, 256], P(('groups', 'fsdp')), may hold values from -0.0625 to 0.0625
- adapter_up_weight: bfloat16 [16, 16384], P('groups', 'fsdp'), may hold values from -1.5 to 1.5
- block_adapter_index: int32 [64], P(('groups', 'fsdp')), may hold values from 0 to 15
- block_valid_length: int32 [64], P(('groups', 'fsdp')), may hold values from 16 to 128
- destinations: int32 [64], P(('groups', 'fsdp')), may hold values from 0 to 31, as said below
- cotangent: bfloat16 [16384, 1024], P(('groups', 'fsdp')), may hold values from -6 to 6
Outputs:
- layer_out: bfloat16 [16384, 1024], P(('groups', 'fsdp'))
- down_gradient: float32 [8192, 256], P(('groups', 'fsdp'))
- up_gradient: float32 [16, 16384], P('groups', 'fsdp')
The draws below stay inside these ranges and needn't reach their ends.
Inputs may be any that keep to these rules, and one draw needn't show every extreme that they name: `destinations`: block j of device d has destination d - 1, d or d + 1; each device sends at most one block to each neighbour.
All inputs are finite; a program needn't handle non-finite values.
Results may differ from the reference program's by a relative error of at most 0.0046.
Values may be sent and summed in bfloat16 or wider, within the bound.
No kernel may reach another device: no remote copies, remote signals or barrier semaphores. Data moves between devices by JAX's collectives and lax.ppermute only.
A program may use at most 128 MiB of HBM per device.

```python
import jax
import jax.numpy as jnp
from jax import lax

MODEL_DIM = 8192
VALUE_WIDTH = 1024
ADAPTER_RANK = 16
ADAPTER_COUNT = 16
BLOCK = 128
BLK_DEV = 2
SLOTS = 4
TOKENS = 8192
BLOCKS = 64
OUT_ROWS = 16384
N_FSDP = 32


def draw_block_valid_length(key, part):
    key = jax.random.fold_in(key, 7)
    lower = max(1, BLOCK // 8)
    drawn = jax.random.randint(key, (BLOCKS,), lower, BLOCK + BLOCK // 4 + 1)
    return jnp.minimum(drawn, BLOCK).astype(jnp.int32)


def draw_destinations(key, part):
    key = jax.random.fold_in(key, 11)
    first_key, another_random_seed = jax.random.split(key)
    right_pick = jax.random.randint(first_key, (N_FSDP,), 0, BLK_DEV + 1)
    left_pick = jax.random.randint(another_random_seed, (N_FSDP,), 0, BLK_DEV + 1)
    device = jnp.arange(N_FSDP, dtype=jnp.int32)
    slot_ids = jnp.arange(BLK_DEV, dtype=jnp.int32)
    go_right = (slot_ids[None, :] == right_pick[:, None]) & (device[:, None] < N_FSDP - 1)
    go_left = (slot_ids[None, :] == left_pick[:, None]) & (left_pick[:, None] != right_pick[:, None]) & (device[:, None] > 0)
    dest_table = device[:, None] + go_right.astype(jnp.int32) - go_left.astype(jnp.int32)
    return dest_table.reshape(-1).astype(jnp.int32)


def place_ends(values, stream_key, smallest, top_value):
    dims = values.shape
    spot = [jax.random.randint(jax.random.fold_in(stream_key, axis), (), 0, dims[axis]) for axis in range(len(dims))]
    values = values.at[tuple(spot)].set(smallest)
    longest = dims.index(max(dims))
    spot[longest] = (spot[longest] + 1) % dims[longest]
    return values.at[tuple(spot)].set(top_value)


def strengthened(values, rng, source, target, shards_of, factor):
    owner, partner = [(jnp.arange(values.shape[axis_at]) // (values.shape[axis_at] // shards_of)).reshape([-1 if axis == axis_at else 1 for axis in range(values.ndim)]) for axis_at in (source, target)]
    chosen = jax.random.permutation(rng, shards_of)[partner]
    strong = (owner == chosen) | (owner == (partner + shards_of // 2) % shards_of)
    return jnp.where(strong, factor * values, values)


def block_levels(rng, dims, shards, smallest, top_value):
    def one(position, shards_of):
        heights = jax.random.uniform(jax.random.fold_in(jax.random.fold_in(rng, 6), position), (shards_of,), jnp.float32, smallest / len(shards), top_value / len(shards))
        return jnp.repeat(jnp.exp(heights), dims[position] // shards_of).reshape((-1,) + (1,) * (len(dims) - position - 1))

    level = one(*shards[0])
    for cut in shards[1:]:
        level = level * one(*cut)
    return level


def scatter_about(rng, dims, deviation, bound, cuts=(), kind=jnp.bfloat16):
    level = block_levels(rng, dims, cuts, -0.22, 0.18) if cuts else 1.0
    values = jax.random.normal(rng, dims, jnp.float32) * deviation * level
    return jnp.minimum(jnp.maximum(values, -bound), bound).astype(kind)


def gaussian_with(rng, dims, scale, bound, cuts, heavy, kind=jnp.bfloat16):
    array = scale * jax.random.normal(rng, dims, jnp.float32)
    if cuts:
        array = array * block_levels(rng, dims, cuts, -0.22, 0.18)
    return jnp.clip(strengthened(array, jax.random.fold_in(rng, 3), *heavy), -bound, bound).astype(kind)


def setup_inputs(seed: int = 0, part: int = 0) -> dict:
    seeds = jax.random.split(jax.random.key(seed), 9)
    own_keys = jax.random.split(jax.random.fold_in(seeds[8], part), 9)
    return {
        "tokens": gaussian_with(own_keys[0], (TOKENS, MODEL_DIM), 1.0, 6.0, ((0, 32),), (0, 1, 32, 2.75)),
        "frozen_value_weight": scatter_about(seeds[1], (MODEL_DIM, VALUE_WIDTH), MODEL_DIM ** -0.5, 0.0625, ((0, 32),)),
        "adapter_down_weight": scatter_about(own_keys[2], (MODEL_DIM, ADAPTER_COUNT * ADAPTER_RANK), MODEL_DIM ** -0.5, 0.0625, ((0, 32),)),
        "adapter_up_weight": scatter_about(own_keys[3], (ADAPTER_RANK, ADAPTER_COUNT * VALUE_WIDTH), ADAPTER_RANK ** -0.5, 1.5, ((1, 32),)),
        "block_adapter_index": place_ends(jax.random.randint(own_keys[4], (BLOCKS,), 0, ADAPTER_COUNT), jax.random.fold_in(own_keys[4], 1), 0, ADAPTER_COUNT - 1).astype(jnp.int32),
        "block_valid_length": draw_block_valid_length(jax.random.fold_in(jax.random.fold_in(seeds[8], part), 71), part),
        "destinations": draw_destinations(jax.random.fold_in(jax.random.fold_in(seeds[8], part), 71), part),
        "cotangent": scatter_about(own_keys[7], (OUT_ROWS, VALUE_WIDTH), 1.0, 6.0, ((0, 32),)),
    }


ADAPTER_SCALE = 2.0


def reference(tokens, frozen_value_weight, adapter_down_weight, adapter_up_weight, block_adapter_index, block_valid_length, destinations, cotangent):
    row_ids = jnp.arange(BLOCK, dtype=jnp.int32)
    valid_row_mask = row_ids[None, :] < block_valid_length[:, None]
    token_blocks = tokens.reshape(BLOCKS, BLOCK, MODEL_DIM)

    def forward_block(inputs):
        block_x, adapter_number, valid_mask = inputs
        base_output = jnp.dot(block_x, frozen_value_weight, preferred_element_type=jnp.float32)
        down_factor = lax.dynamic_slice_in_dim(adapter_down_weight, (adapter_number * ADAPTER_RANK).astype(jnp.int32), ADAPTER_RANK, 1)
        activation_matrix = jnp.dot(block_x, down_factor, preferred_element_type=jnp.float32).astype(jnp.bfloat16)
        up_weight_columns = lax.dynamic_slice_in_dim(adapter_up_weight, (adapter_number * VALUE_WIDTH).astype(jnp.int32), VALUE_WIDTH, 1)
        adapter_output = jnp.dot(activation_matrix, up_weight_columns, preferred_element_type=jnp.float32)
        value_output = jnp.where(valid_mask[:, None], base_output + ADAPTER_SCALE * adapter_output, jnp.float32(0.0)).astype(jnp.bfloat16)
        return value_output, activation_matrix

    block_out, block_hidden = lax.map(forward_block, (token_blocks, block_adapter_index, valid_row_mask))

    dest_table = destinations.reshape(N_FSDP, BLK_DEV)
    device = jnp.arange(N_FSDP, dtype=jnp.int32)[:, None]
    slot_ids = jnp.arange(BLK_DEV, dtype=jnp.int32)[None, :]
    goes_right = dest_table == device + 1
    goes_left = dest_table == device - 1
    stays = dest_table == device
    first_block = device[:, 0] * BLK_DEV
    right_source = first_block + jnp.sum(jnp.where(goes_right, slot_ids, 0), axis=1).astype(jnp.int32)
    left_source = first_block + jnp.sum(jnp.where(goes_left, slot_ids, 0), axis=1).astype(jnp.int32)
    has_right = jnp.any(goes_right, axis=1)
    has_left = jnp.any(goes_left, axis=1)
    from_lower = jnp.roll(right_source, 1)
    lower_valid = jnp.roll(has_right, 1)
    from_upper = jnp.roll(left_source, -1)
    upper_valid = jnp.roll(has_left, -1)
    own_source = (device * BLK_DEV + slot_ids).astype(jnp.int32)
    source_table = jnp.concatenate([from_lower[:, None], own_source, from_upper[:, None]], axis=1).astype(jnp.int32)
    valid_table = jnp.concatenate([lower_valid[:, None], stays, upper_valid[:, None]], axis=1)
    positioned_entries = block_out[source_table.reshape(-1)]
    layer_out = jnp.where(valid_table.reshape(-1)[:, None, None], positioned_entries, jnp.zeros((), jnp.bfloat16)).reshape(-1, VALUE_WIDTH)

    landing = jnp.where(goes_right, (device + 1) * SLOTS,
                        jnp.where(goes_left, (device - 1) * SLOTS + SLOTS - 1, device * SLOTS + 1 + slot_ids))
    landing = landing.reshape(-1).astype(jnp.int32)
    slot_grad = cotangent.reshape(-1, BLOCK, VALUE_WIDTH)
    block_grad = jnp.where(valid_row_mask[..., None], slot_grad[landing], jnp.zeros((), jnp.bfloat16))

    adapter_selector = (block_adapter_index[:, None] == jnp.arange(ADAPTER_COUNT, dtype=jnp.int32)[None, :]).astype(jnp.float32)
    up_weight_terms = jnp.einsum("bnr,bnk->brk", block_hidden.astype(jnp.float32), block_grad.astype(jnp.float32))
    up_gradient = ADAPTER_SCALE * jnp.einsum("yo,yqg->qog", adapter_selector, up_weight_terms, precision=lax.Precision.HIGHEST)
    up_gradient = up_gradient.reshape(ADAPTER_RANK, ADAPTER_COUNT * VALUE_WIDTH)

    def accumulate(loop_carry, inputs):
        block_x, block_g, adapter_number = inputs
        up_weight_columns = lax.dynamic_slice_in_dim(adapter_up_weight, (adapter_number * VALUE_WIDTH).astype(jnp.int32), VALUE_WIDTH, 1)
        low_grad = jnp.dot(block_g, up_weight_columns.T, preferred_element_type=jnp.float32).astype(jnp.bfloat16)
        term = jnp.dot(block_x.T, low_grad, preferred_element_type=jnp.float32)
        return loop_carry.at[adapter_number].add(term), None

    loop_carry, unused = lax.scan(accumulate, jnp.zeros((ADAPTER_COUNT, MODEL_DIM, ADAPTER_RANK), jnp.float32),
                             (token_blocks, block_grad, block_adapter_index))
    down_gradient = ADAPTER_SCALE * jnp.transpose(loop_carry, (1, 0, 2)).reshape(MODEL_DIM, ADAPTER_COUNT * ADAPTER_RANK)
    return layer_out, down_gradient, up_gradient
```

```python
import functools

import jax
import jax.numpy as jnp
from jax import lax
from jax.experimental import pallas as pl
from jax.experimental.pallas import tpu as pltpu
from jax.sharding import PartitionSpec as P

RANK = 16
COUNT = 16
BLOCK = 128
WIDE = RANK * COUNT
SCALE = 2.0
MIB = 1 << 20
F32 = jnp.float32
BF16 = jnp.bfloat16
VMEM = pl.BlockSpec(memory_space=pltpu.VMEM)
ANY = pl.BlockSpec(memory_space=pl.ANY)


def send_to(x, size, target):
    return lax.ppermute(x, "fsdp", [(i, target(i)) for i in range(size)])


def swap(x, size, bit):
    return send_to(x, size, lambda i: i ^ bit)


def ring(x, size):
    return send_to(x, size, lambda i: (i + 8) % size)


def shift(x, size, step):
    pairs = [(i, i + step) for i in range(size) if 0 <= i + step < size]
    return lax.ppermute(x, "fsdp", pairs)


def chip_at(me, planes, group, step):
    chip = me // 2
    z = chip // 4
    y = (chip // 2) % 2
    x = chip % 2
    if group & 1:
        x = 1 - x
    if group & 2:
        y = 1 - y
    return lax.rem(z + planes - step, planes) * 4 + y * 2 + x


def gather_pieces(piece, size):
    held = [piece]
    for _ in range(size // 8 - 1):
        held.append(ring(held[-1], size))
    line = jnp.stack(held)
    half = line.shape[0] // 2
    across_x = swap(line, size, 2)
    across_y = swap(line, size, 4)
    first = swap(across_x[:half], size, 4)
    last = swap(across_y[half:], size, 2)
    return line, across_x, across_y, first, last


def split_tokens(tokens, size):
    rows, width = tokens.shape
    depth = width // size
    chips = size // 2
    planes = size // 8

    def kernel(tok, mine, other, sems):
        me = lax.axis_index("fsdp")
        core = lax.rem(me, 2)
        copies = []
        for i in range(chips):
            chip = chip_at(me, planes, i // planes, i % planes)
            for n, (ref, parity) in enumerate(((other, 1 - core), (mine, core))):
                start = pl.multiple_of((2 * chip + parity) * depth, depth)
                copy = pltpu.make_async_copy(
                    tok.at[:, pl.ds(start, depth)],
                    ref.at[:, pl.ds(i * depth, depth)],
                    sems.at[n, i],
                )
                copy.start()
                copies.append(copy)
        for copy in copies:
            copy.wait()

    half = jax.ShapeDtypeStruct((rows, width // 2), tokens.dtype)
    return pl.pallas_call(
        kernel,
        out_shape=(half, half),
        in_specs=[ANY],
        out_specs=(ANY, ANY),
        scratch_shapes=[pltpu.SemaphoreType.DMA((2, chips))],
        name="split_tokens",
    )(tokens)


def dot(a, b):
    return jnp.dot(a, b, preferred_element_type=F32)


def dot_nt(a, b):
    return lax.dot_general(a, b, (((1,), (1,)), ((), ())), preferred_element_type=F32)


def dot_tn(a, b):
    return lax.dot_general(a, b, (((0,), (0,)), ((), ())), preferred_element_type=F32)


def low_rank_products(tok, tok_in, pieces, grad, grad_in, size):
    rows = tok.shape[0]
    depth = tok.shape[1] * 2 // size
    planes = size // 8
    quarters = (pieces[0].shape[1] - depth - 16) // 16

    def kernel(tok, tok_in, line, ax, ay, first, last, grad, grad_in, out, table):
        me = lax.axis_index("fsdp")

        def piece(i):
            group, step = i // planes, i % planes
            if group < 3:
                return (line, ax, ay)[group].at[step]
            return first.at[step] if step < planes // 2 else last.at[step - planes // 2]

        for half, source in enumerate((tok, tok_in)):
            total = jnp.zeros((rows, WIDE), F32)
            for i in range(4 * planes):
                total += dot(source[:, i * depth : (i + 1) * depth], piece(i)[:depth])
            out[half * rows : (half + 1) * rows] = total
        meta = jnp.zeros((16, WIDE), F32)
        for i in range(4 * planes):
            chip = chip_at(me, planes, i // planes, i % planes)
            for q in range(quarters):
                flat = chip * quarters + q
                spot = pl.multiple_of(flat // 2 * RANK, RANK)
                table[lax.rem(flat, 2), pl.ds(spot, RANK), :] = piece(i)[
                    depth + q * 16 : depth + (q + 1) * 16
                ]
            meta += piece(i)[depth + quarters * 16 :].astype(F32)
        for half, source in enumerate((grad, grad_in)):
            low = dot_nt(source[:, :256], table[0]) + dot_nt(source[:, 256:], table[1])
            out[(2 + half) * rows : (3 + half) * rows] = low
        out[4 * rows :] = meta

    return pl.pallas_call(
        kernel,
        out_shape=(
            jax.ShapeDtypeStruct((4 * rows + 16, WIDE), F32),
            jax.ShapeDtypeStruct((2, WIDE, 256), BF16),
        ),
        in_specs=[VMEM] * 9,
        out_specs=(VMEM, VMEM),
        compiler_params=pltpu.CompilerParams(vmem_limit_bytes=20 * MIB),
        cost_estimate=pl.CostEstimate(
            flops=4 * rows * (tok.shape[1] + 512) * WIDE, bytes_accessed=9 * MIB, transcendentals=0
        ),
        name="low_rank_products",
    )(tok, tok_in, *pieces, grad, grad_in)


def adapter_terms(own, other, tok, tok_in, grad, grad_in, size, kind):
    rows = tok.shape[0]
    depth = tok.shape[1] * 2 // size
    planes = size // 8
    slices = 512 // depth

    def kernel(own, other, tok, tok_in, grad, grad_in, hidden, names, terms):
        me = lax.axis_index("fsdp")
        table = own[4 * rows :] + other[4 * rows :]
        names[...] = table
        lane = lax.broadcasted_iota(jnp.int32, (1, WIDE), 1)
        row = lax.broadcasted_iota(jnp.int32, (rows, 1), 0)
        adapter_of_lane = (lane // RANK).astype(F32)
        fold_row = lax.broadcasted_iota(jnp.int32, (WIDE, 2 * RANK), 0)
        fold_lane = lax.broadcasted_iota(jnp.int32, (WIDE, 2 * RANK), 1)
        fold = (fold_row % RANK == fold_lane % RANK).astype(F32).astype(BF16)
        block_lane = lax.broadcasted_iota(jnp.int32, (rows, 2 * RANK), 1) // RANK
        block_row = lax.broadcasted_iota(jnp.int32, (rows, 2 * RANK), 0) // BLOCK
        for half, source in enumerate((tok, tok_in)):
            device = me if half == 0 else me + 1 - 2 * lax.rem(me, 2)
            found = [
                jnp.sum(jnp.where(lane == device, table[b : b + 1], 0.0), axis=1, keepdims=True)
                for b in range(2)
            ]
            adapter = jnp.where(row < BLOCK, found[0], found[1])
            chosen = adapter_of_lane == adapter
            mine, theirs = half * rows, (1 - half) * rows
            act = own[mine : mine + rows] + other[theirs : theirs + rows]
            hidden[mine : mine + rows] = jnp.where(chosen, act, 0.0).astype(BF16)
            mine, theirs = mine + 2 * rows, theirs + 2 * rows
            low = own[mine : mine + rows] + other[theirs : theirs + rows]
            low = jnp.where(chosen, low, 0.0).astype(BF16)
            narrow = jnp.where(block_lane == block_row, dot(low, fold), 0.0).astype(BF16)
            for i in range(4 * planes):
                chip = chip_at(me, planes, i // planes, i % planes)
                term = dot_tn(narrow, source[:, i * depth : (i + 1) * depth])
                terms[chip, half * 32 : (half + 1) * 32, :] = term.astype(kind)
        up = dot_tn(hidden[:rows], grad[...]) + dot_tn(hidden[rows:], grad_in[...])
        for a in range(COUNT):
            for t in range(slices):
                chip, place = divmod(a * slices + t, 2)
                terms[chip, 64 + 16 * place : 80 + 16 * place, :] = up[
                    a * RANK : (a + 1) * RANK, t * depth : (t + 1) * depth
                ].astype(kind)

    return pl.pallas_call(
        kernel,
        out_shape=(
            jax.ShapeDtypeStruct((2 * rows, WIDE), BF16),
            jax.ShapeDtypeStruct((16, WIDE), F32),
            jax.ShapeDtypeStruct((size // 2, 96, depth), kind),
        ),
        in_specs=[VMEM] * 6,
        out_specs=(VMEM, VMEM, VMEM),
        compiler_params=pltpu.CompilerParams(vmem_limit_bytes=24 * MIB),
        cost_estimate=pl.CostEstimate(
            flops=4 * rows * tok.shape[1] * 128, bytes_accessed=9 * MIB, transcendentals=0
        ),
        name="adapter_terms",
    )(own, other, tok, tok_in, grad, grad_in)


def sum_terms(terms, names, size):
    chips, _, depth = terms.shape

    def kernel(terms, names, down, up):
        core = lax.rem(lax.axis_index("fsdp"), 2)
        count = chips * 64
        device = lax.broadcasted_iota(jnp.int32, (WIDE, count), 0)
        spot = lax.broadcasted_iota(jnp.int32, (WIDE, count), 1)
        block = (spot // 16) % 4
        sender = 2 * (spot // 64) + jnp.where(block < 2, core, 1 - core)
        table = names[...].astype(BF16)
        first = ((device == sender) & (block % 2 == 0)).astype(F32).astype(BF16)
        second = ((device == sender) & (block % 2 == 1)).astype(F32).astype(BF16)
        adapter = (dot(table, first)[0:1] + dot(table, second)[1:2]).astype(jnp.int32)
        pick = (device == adapter * RANK + spot % RANK).astype(F32)
        source = terms[:, :64, :].reshape(count, depth)
        if terms.dtype == BF16:
            total = dot(pick.astype(BF16), source)
        else:
            total = jnp.dot(
                pick, source, preferred_element_type=F32, precision=lax.Precision.HIGHEST
            )
        down[...] = SCALE * total.T
        for s in range(2):
            up[:, s * depth : (s + 1) * depth] = SCALE * jnp.sum(
                terms[:, 64 + 16 * s : 80 + 16 * s, :].astype(F32), axis=0
            )

    return pl.pallas_call(
        kernel,
        out_shape=(
            jax.ShapeDtypeStruct((depth, WIDE), F32),
            jax.ShapeDtypeStruct((RANK, 2 * depth), F32),
        ),
        in_specs=[VMEM] * 2,
        out_specs=(VMEM, VMEM),
        compiler_params=pltpu.CompilerParams(vmem_limit_bytes=24 * MIB),
        cost_estimate=pl.CostEstimate(
            flops=2 * WIDE * chips * 64 * depth, bytes_accessed=2 * MIB, transcendentals=0
        ),
        name="sum_terms",
    )(terms, names)


def value_products(tok, tok_in, pieces, hidden, table, start, size):
    rows = tok.shape[0]
    depth = tok.shape[1] * 2 // size
    planes = size // 8
    columns = pieces[0].shape[2]
    own_columns = 2 * depth

    def kernel(tok, tok_in, line, ax, ay, first, last, hidden, table, keep, give):
        core = lax.rem(lax.axis_index("fsdp"), 2)
        for half, (source, out) in enumerate(((tok, keep), (tok_in, give))):
            for m in range(columns // 256):
                here = slice(m * 256, (m + 1) * 256)
                begin = 0
                total = None
                for ref in (line, ax, ay, first, last):
                    deep = ref.shape[0] * depth
                    part = dot(
                        source[:, begin : begin + deep], ref[:, :, here].reshape(deep, 256)
                    )
                    total = part if total is None else total + part
                    begin += deep
                column = start + m * 256
                owner = column // own_columns
                q = (owner // 2 * own_columns + column % own_columns) // 256
                scale = jnp.where(core == owner % 2, SCALE, 0.0).astype(F32)
                extra = dot(hidden[half * rows : (half + 1) * rows], table[q])
                out[:, here] = total + scale * extra

    share = jax.ShapeDtypeStruct((rows, columns), F32)
    return pl.pallas_call(
        kernel,
        out_shape=(share, share),
        in_specs=[VMEM] * 9,
        out_specs=(VMEM, VMEM),
        compiler_params=pltpu.CompilerParams(vmem_limit_bytes=20 * MIB),
        cost_estimate=pl.CostEstimate(
            flops=4 * rows * tok.shape[1] * columns, bytes_accessed=9 * MIB, transcendentals=0
        ),
        name="value_products",
    )(tok, tok_in, *pieces, hidden, table)


def body(
    size,
    tokens,
    frozen_value_weight,
    adapter_down_weight,
    adapter_up_weight,
    block_adapter_index,
    block_valid_length,
    destinations,
    cotangent,
):
    width = frozen_value_weight.shape[1]
    own_columns = adapter_up_weight.shape[1]
    me = lax.axis_index("fsdp")
    core = me % 2
    goes_right = (destinations == me + 1)[:, None, None]
    goes_left = (destinations == me - 1)[:, None, None]
    stays = (destinations == me)[:, None, None]
    valid = (jnp.arange(BLOCK)[None, :] < block_valid_length[:, None])[..., None]
    zero = jnp.zeros((), BF16)

    lane = jnp.arange(WIDE)[None, :]
    meta = jnp.where(lane == me, block_adapter_index[:, None], 0).astype(BF16)
    meta = jnp.concatenate([meta, jnp.zeros((14, WIDE), BF16)])
    ups = [adapter_up_weight[:, q * 256 : (q + 1) * 256] for q in range(own_columns // 256)]
    piece = jnp.concatenate([adapter_down_weight, *ups, meta])
    low_pieces = gather_pieces(piece, size)

    tok, tok_out = split_tokens(tokens, size)
    tok_in = swap(tok_out, size, 1)

    slots = cotangent.reshape(-1, BLOCK, width)
    from_upper = shift(slots[0], size, -1)
    from_lower = shift(slots[-1], size, 1)
    grad = jnp.where(goes_right, from_upper[None], jnp.where(goes_left, from_lower[None], slots[1:-1]))
    grad = jnp.where(valid, grad, zero).reshape(-1, width)
    runs = [grad[:, i : i + own_columns] for i in range(0, width, own_columns)]
    even, odd = jnp.concatenate(runs[0::2], axis=1), jnp.concatenate(runs[1::2], axis=1)
    grad_mine = jnp.where(core == 0, even, odd)
    grad_in = swap(jnp.where(core == 0, odd, even), size, 1)

    share, table = low_rank_products(tok, tok_in, low_pieces, grad_mine, grad_in, size)
    hidden, names, terms = adapter_terms(
        share, swap(share, size, 1), tok, tok_in, grad_mine, grad_in, size, F32
    )
    groups = [list(range(core, size, 2)) for core in range(2)]
    terms = lax.all_to_all(terms, "fsdp", 0, 0, axis_index_groups=groups, tiled=True)
    down_gradient, up_gradient = sum_terms(terms, names, size)

    outs = []
    for start, stop in ((0, 512), (512, 1024)):
        pieces = gather_pieces(frozen_value_weight[:, start:stop], size)
        keep, give = value_products(tok, tok_in, pieces, hidden, table, start, size)
        total = (keep + swap(give, size, 1)).reshape(-1, BLOCK, stop - start)
        value = jnp.where(valid, total, 0.0).astype(BF16)
        right = jnp.sum(jnp.where(goes_right, value, zero), axis=0)
        left = jnp.sum(jnp.where(goes_left, value, zero), axis=0)
        own = jnp.where(stays, value, zero)
        lower, upper = shift(right, size, 1), shift(left, size, -1)
        outs.append(jnp.concatenate([lower[None], own, upper[None]]).reshape(-1, stop - start))
    return jnp.concatenate(outs, axis=1), down_gradient, up_gradient


def solution(mesh):
    rows = P(("groups", "fsdp"), None)
    vector = P(("groups", "fsdp"))
    in_specs = (rows, P("fsdp", None), rows, P("groups", "fsdp"), vector, vector, vector, rows)
    out_specs = (rows, rows, P("groups", "fsdp"))
    return jax.shard_map(
        functools.partial(body, mesh.shape["fsdp"]),
        mesh=mesh,
        in_specs=in_specs,
        out_specs=out_specs,
        check_vma=False,
    )
```

```python
import functools

import jax
import jax.numpy as jnp
from jax import lax
from jax.experimental import pallas as pl
from jax.experimental.pallas import tpu as pltpu
from jax.sharding import PartitionSpec as P

RANK = 16
COUNT = 16
BLOCK = 128
WIDE = RANK * COUNT
SCALE = 2.0
MIB = 1 << 20
F32 = jnp.float32
BF16 = jnp.bfloat16
VMEM = pl.BlockSpec(memory_space=pltpu.VMEM)
ANY = pl.BlockSpec(memory_space=pl.ANY)


def send_to(x, size, target):
    return lax.ppermute(x, "fsdp", [(i, target(i)) for i in range(size)])


def swap(x, size, bit):
    return send_to(x, size, lambda i: i ^ bit)


def turn(x, size, planes):
    return send_to(x, size, lambda i: (i + 8 * planes) % size)


def shift(x, size, step):
    pairs = [(i, i + step) for i in range(size) if 0 <= i + step < size]
    return lax.ppermute(x, "fsdp", pairs)


def chip_at(me, planes, group, step):
    chip = me // 2
    z = chip // 4
    y = (chip // 2) % 2
    x = chip % 2
    if group & 1:
        x = 1 - x
    if group & 2:
        y = 1 - y
    return lax.rem(z + planes - step, planes) * 4 + y * 2 + x


def ordered(x, *before):
    return lax.optimization_barrier((x, *before))[0]


class Rows:
    def __init__(self, array, parts):
        self.array = array
        self.parts = parts

    def part(self, kind, begin, count):
        if not count:
            return None
        parts, row, seen, first = [], 0, 0, None
        for k, group, step, at, n in self.parts:
            if k == kind and group in (1, 2):
                low, high = max(begin, seen), min(begin + count, seen + n)
                if low < high:
                    parts.append((k, group, step, at + low - seen, high - low))
                    first = row + low - seen if first is None else first
                seen += n
            row += n
        return Rows(self.array[first : first + count], parts)

    def count(self, kind):
        return sum(n for k, group, _, _, n in self.parts if k == kind and group in (1, 2))

    def swapped(self, size, group):
        parts = [(k, g ^ group, s, at, n) for k, g, s, at, n in self.parts]
        return Rows(swap(self.array, size, 2 * group), parts)

    def turned(self, size, planes):
        parts = [(k, g, s + planes, at, n) for k, g, s, at, n in self.parts]
        return Rows(turn(self.array, size, planes), parts)


def joined(rows):
    rows = [r for r in rows if r is not None]
    if len(rows) == 1:
        return rows[0]
    return Rows(jnp.concatenate([r.array for r in rows]), [p for r in rows for p in r.parts])


def halves(rows, kind, unit):
    total = rows.count(kind)
    cut = total // 2 // unit * unit
    return cut, total - cut


def across(line, previous, kinds, size):
    by_x, by_y = list(line), list(line)
    if previous is not None:
        over_x, over_y = previous
        for kind, unit in kinds:
            cut, rest = halves(over_x, kind, unit)
            by_y.append(over_x.part(kind, 0, cut))
            by_x.append(over_y.part(kind, cut, rest))
    sent = [joined(rows) for rows in (by_x, by_y) if any(r is not None for r in rows)]
    return sent, [rows.swapped(size, 1 + (i == len(sent) - 1)) for i, rows in enumerate(sent)]


def split_tokens(tokens, size):
    rows, width = tokens.shape
    depth = width // size
    chips = size // 2
    planes = size // 8

    def kernel(tok, mine, other):
        me = lax.axis_index("fsdp")
        core = lax.rem(me, 2)
        for i in range(chips):
            chip = chip_at(me, planes, i // planes, i % planes)
            for ref, parity in ((other, 1 - core), (mine, core)):
                start = pl.multiple_of((2 * chip + parity) * depth, depth)
                ref[:, i * depth : (i + 1) * depth] = tok[:, pl.ds(start, depth)]

    half = jax.ShapeDtypeStruct((rows, width // 2), tokens.dtype)
    return pl.pallas_call(
        kernel,
        out_shape=(half, half),
        in_specs=[VMEM],
        out_specs=(VMEM, VMEM),
        compiler_params=pltpu.CompilerParams(vmem_limit_bytes=16 * MIB),
        cost_estimate=pl.CostEstimate(flops=0, bytes_accessed=4 * rows * width, transcendentals=0),
        name="split_tokens",
    )(tokens)


def dot(a, b):
    return jnp.dot(a, b, preferred_element_type=F32)


def dot_nt(a, b):
    return lax.dot_general(a, b, (((1,), (1,)), ((), ())), preferred_element_type=F32)


def dot_tn(a, b):
    return lax.dot_general(a, b, (((0,), (0,)), ((), ())), preferred_element_type=F32)


def low_rank_products(tok, tok_in, pieces, grad, grad_in, size, after):
    rows = tok.shape[0]
    depth = tok.shape[1] * 2 // size
    planes = size // 8
    deep = depth // 4
    quarters = 2 * depth // 256
    count = len(pieces)

    def kernel(tok, tok_in, *refs):
        refs, (grad, grad_in), (out, table, down) = refs[:count], refs[count : count + 2], refs[-3:]
        me = lax.axis_index("fsdp")
        meta = jnp.zeros((16, WIDE), F32)
        for ref, piece in zip(refs, pieces):
            row = 0
            for kind, group, step, at, n in piece.parts:
                begin, row = row, row + n
                if kind != "low":
                    continue
                spot = group * planes + step
                n_down = min(n, deep - at)
                if n_down > 0:
                    for g in range(4):
                        to = spot * depth + g * deep + at
                        down[to : to + n_down] = ref[begin : begin + n_down, g * 256 : (g + 1) * 256]
                if at + n <= deep:
                    continue
                last = slice(row - 16, row)
                chip = chip_at(me, planes, group, step)
                for q in range(quarters):
                    flat = chip * quarters + q
                    to = pl.multiple_of(flat // 2 * RANK, RANK)
                    table[lax.rem(flat, 2), pl.ds(to, RANK), :] = ref[last, q * 256 : (q + 1) * 256]
                meta += ref[last, 512 : 512 + WIDE].astype(F32)
        for half, source in enumerate((tok, tok_in)):
            out[half * rows : (half + 1) * rows] = dot(source[...], down[...])
        for half, source in enumerate((grad, grad_in)):
            low = dot_nt(source[:, :256], table[0]) + dot_nt(source[:, 256:], table[1])
            out[(2 + half) * rows : (3 + half) * rows] = low
        out[4 * rows :] = meta

    return pl.pallas_call(
        kernel,
        out_shape=(
            jax.ShapeDtypeStruct((4 * rows + 16, WIDE), F32),
            jax.ShapeDtypeStruct((2, WIDE, 256), BF16),
        ),
        in_specs=[VMEM] * (4 + count) + [ANY] * len(after),
        out_specs=(VMEM, VMEM),
        scratch_shapes=[pltpu.VMEM((tok.shape[1], WIDE), BF16)],
        compiler_params=pltpu.CompilerParams(vmem_limit_bytes=24 * MIB),
        cost_estimate=pl.CostEstimate(
            flops=4 * rows * (tok.shape[1] + 512) * WIDE, bytes_accessed=9 * MIB, transcendentals=0
        ),
        name="low_rank_products",
    )(tok, tok_in, *(p.array for p in pieces), grad, grad_in, *after)


def adapter_terms(own, other, tok, tok_in, grad, grad_in, size, kind):
    rows = tok.shape[0]
    depth = tok.shape[1] * 2 // size
    planes = size // 8
    slices = 512 // depth

    def kernel(own, other, tok, tok_in, grad, grad_in, hidden, names, terms):
        me = lax.axis_index("fsdp")
        table = own[4 * rows :] + other[4 * rows :]
        names[...] = table
        lane = lax.broadcasted_iota(jnp.int32, (1, WIDE), 1)
        row = lax.broadcasted_iota(jnp.int32, (rows, 1), 0)
        adapter_of_lane = (lane // RANK).astype(F32)
        fold_row = lax.broadcasted_iota(jnp.int32, (WIDE, 2 * RANK), 0)
        fold_lane = lax.broadcasted_iota(jnp.int32, (WIDE, 2 * RANK), 1)
        fold = (fold_row % RANK == fold_lane % RANK).astype(F32).astype(BF16)
        block_lane = lax.broadcasted_iota(jnp.int32, (rows, 2 * RANK), 1) // RANK
        block_row = lax.broadcasted_iota(jnp.int32, (rows, 2 * RANK), 0) // BLOCK
        for half, source in enumerate((tok, tok_in)):
            device = me if half == 0 else me + 1 - 2 * lax.rem(me, 2)
            found = [
                jnp.sum(jnp.where(lane == device, table[b : b + 1], 0.0), axis=1, keepdims=True)
                for b in range(2)
            ]
            adapter = jnp.where(row < BLOCK, found[0], found[1])
            chosen = adapter_of_lane == adapter
            mine, theirs = half * rows, (1 - half) * rows
            act = own[mine : mine + rows] + other[theirs : theirs + rows]
            hidden[mine : mine + rows] = jnp.where(chosen, act, 0.0).astype(BF16)
            mine, theirs = mine + 2 * rows, theirs + 2 * rows
            low = own[mine : mine + rows] + other[theirs : theirs + rows]
            low = jnp.where(chosen, low, 0.0).astype(BF16)
            narrow = jnp.where(block_lane == block_row, dot(low, fold), 0.0).astype(BF16)
            for i in range(4 * planes):
                chip = chip_at(me, planes, i // planes, i % planes)
                term = dot_tn(narrow, source[:, i * depth : (i + 1) * depth])
                terms[chip, half * 32 : (half + 1) * 32, :] = term.astype(kind)
        up = dot_tn(hidden[:rows], grad[...]) + dot_tn(hidden[rows:], grad_in[...])
        for a in range(COUNT):
            for t in range(slices):
                chip, place = divmod(a * slices + t, 2)
                terms[chip, 64 + 16 * place : 80 + 16 * place, :] = up[
                    a * RANK : (a + 1) * RANK, t * depth : (t + 1) * depth
                ].astype(kind)

    return pl.pallas_call(
        kernel,
        out_shape=(
            jax.ShapeDtypeStruct((2 * rows, WIDE), BF16),
            jax.ShapeDtypeStruct((16, WIDE), F32),
            jax.ShapeDtypeStruct((size // 2, 96, depth), kind),
        ),
        in_specs=[VMEM] * 6,
        out_specs=(VMEM, VMEM, VMEM),
        compiler_params=pltpu.CompilerParams(vmem_limit_bytes=24 * MIB),
        cost_estimate=pl.CostEstimate(
            flops=4 * rows * tok.shape[1] * 128, bytes_accessed=9 * MIB, transcendentals=0
        ),
        name="adapter_terms",
    )(own, other, tok, tok_in, grad, grad_in)


def sum_terms(terms, names, size):
    chips, _, depth = terms.shape

    def kernel(terms, names, down, up):
        core = lax.rem(lax.axis_index("fsdp"), 2)
        count = chips * 64
        device = lax.broadcasted_iota(jnp.int32, (WIDE, count), 0)
        spot = lax.broadcasted_iota(jnp.int32, (WIDE, count), 1)
        block = (spot // 16) % 4
        sender = 2 * (spot // 64) + jnp.where(block < 2, core, 1 - core)
        table = names[...].astype(BF16)
        first = ((device == sender) & (block % 2 == 0)).astype(F32).astype(BF16)
        second = ((device == sender) & (block % 2 == 1)).astype(F32).astype(BF16)
        adapter = (dot(table, first)[0:1] + dot(table, second)[1:2]).astype(jnp.int32)
        pick = (device == adapter * RANK + spot % RANK).astype(F32)
        source = terms[:, :64, :].reshape(count, depth)
        if terms.dtype == BF16:
            total = dot(pick.astype(BF16), source)
        else:
            total = jnp.dot(
                pick, source, preferred_element_type=F32, precision=lax.Precision.HIGHEST
            )
        down[...] = SCALE * total.T
        for s in range(2):
            up[:, s * depth : (s + 1) * depth] = SCALE * jnp.sum(
                terms[:, 64 + 16 * s : 80 + 16 * s, :].astype(F32), axis=0
            )

    return pl.pallas_call(
        kernel,
        out_shape=(
            jax.ShapeDtypeStruct((depth, WIDE), F32),
            jax.ShapeDtypeStruct((RANK, 2 * depth), F32),
        ),
        in_specs=[VMEM] * 2,
        out_specs=(VMEM, VMEM),
        compiler_params=pltpu.CompilerParams(vmem_limit_bytes=24 * MIB),
        cost_estimate=pl.CostEstimate(
            flops=2 * WIDE * chips * 64 * depth, bytes_accessed=2 * MIB, transcendentals=0
        ),
        name="sum_terms",
    )(terms, names)


def value_products(tok, tok_in, pieces, so_far, adapters, size, after):
    rows = tok.shape[0]
    depth = tok.shape[1] * 2 // size
    planes = size // 8
    own_columns = 2 * depth
    width = pieces[0].array.shape[1]
    count = len(pieces)
    terms = []
    for n, piece in enumerate(pieces):
        row = 0
        for kind, group, step, at, height in piece.parts:
            if kind == "wide":
                terms.append((n, row, (group * planes + step) * depth + at, height))
            row += height
    joint = so_far or adapters

    def kernel(tok, tok_in, *refs):
        refs, joint, (keep, give) = refs[:count], refs[count : count + 2], refs[-2:]
        core = lax.rem(lax.axis_index("fsdp"), 2)
        for half, (source, out) in enumerate(((tok, keep), (tok_in, give))):
            for left in range(0, width, 256):
                here = slice(left, left + 256)
                if so_far:
                    total = joint[half][:, here]
                else:
                    owner = left // own_columns
                    place = (owner // 2 * own_columns + left % own_columns) // 256
                    scale = jnp.where(core == owner % 2, SCALE, 0.0).astype(F32)
                    total = scale * dot(joint[0][half * rows : (half + 1) * rows], joint[1][place])
                for n, row, spot, height in terms:
                    total += dot(source[:, spot : spot + height], refs[n][row : row + height, here])
                out[:, here] = total

    share = jax.ShapeDtypeStruct((rows, width), F32)
    return pl.pallas_call(
        kernel,
        out_shape=(share, share),
        in_specs=[VMEM] * (4 + count) + [ANY] * len(after),
        out_specs=(VMEM, VMEM),
        compiler_params=pltpu.CompilerParams(vmem_limit_bytes=28 * MIB),
        cost_estimate=pl.CostEstimate(
            flops=4 * rows * sum(t[3] for t in terms) * width,
            bytes_accessed=4 * MIB,
            transcendentals=0,
        ),
        name="value_products",
    )(tok, tok_in, *(p.array for p in pieces), *joint, *after)


def body(
    size,
    tokens,
    frozen_value_weight,
    adapter_down_weight,
    adapter_up_weight,
    block_adapter_index,
    block_valid_length,
    destinations,
    cotangent,
):
    width = frozen_value_weight.shape[1]
    own_columns = adapter_up_weight.shape[1]
    me = lax.axis_index("fsdp")
    core = me % 2
    goes_right = (destinations == me + 1)[:, None, None]
    goes_left = (destinations == me - 1)[:, None, None]
    stays = (destinations == me)[:, None, None]
    valid = (jnp.arange(BLOCK)[None, :] < block_valid_length[:, None])[..., None]
    zero = jnp.zeros((), BF16)

    depth = adapter_down_weight.shape[0]
    deep = depth // 4
    planes = size // 8
    lane = jnp.arange(WIDE)[None, :]
    meta = jnp.where(lane == me, block_adapter_index[:, None], 0).astype(BF16)
    meta = jnp.pad(meta, ((0, 14), (0, 0)))
    downs = [adapter_down_weight[g * deep : (g + 1) * deep] for g in range(4)]
    ups = jnp.pad(adapter_up_weight, ((0, 0), (0, 512 - own_columns)))
    last_rows = jnp.concatenate([ups, meta, jnp.zeros_like(meta)], axis=1)
    low_piece = jnp.concatenate([jnp.concatenate(downs, axis=1), last_rows])
    low = [Rows(low_piece, [("low", 0, 0, 0, deep + 16)])]
    wide = [Rows(frozen_value_weight, [("wide", 0, 0, 0, depth)])]
    kinds = (("wide", 128), ("low", 16))

    low += [low[0].turned(size, step) for step in range(1, planes)]
    wide[0].array = ordered(wide[0].array, *(r.array for r in low[1:]))
    for step in range(planes - 1):
        wide.append(wide[-1].turned(size, 1))
    _, stage0 = across([Rows(frozen_value_weight, wide[0].parts), low[0]], None, kinds, size)
    _, stage1 = across(low[1:], stage0, kinds, size)
    _, stage2 = across([wide[1]], stage1, kinds, size)
    sent, stage = across([wide[2]], stage2, kinds, size)
    stages = [stage0, stage1, stage2, stage]

    tok, tok_out = split_tokens(tokens, size)
    tok_in = swap(tok_out, size, 1)

    slots = cotangent.reshape(-1, BLOCK, width)
    from_upper = shift(slots[0], size, -1)
    from_lower = shift(slots[-1], size, 1)
    grad = jnp.where(goes_right, from_upper[None], jnp.where(goes_left, from_lower[None], slots[1:-1]))
    grad = jnp.where(valid, grad, zero).reshape(-1, width)
    runs = [grad[:, i : i + own_columns] for i in range(0, width, own_columns)]
    even, odd = jnp.concatenate(runs[0::2], axis=1), jnp.concatenate(runs[1::2], axis=1)
    grad_mine = jnp.where(core == 0, even, odd)
    grad_in = swap(jnp.where(core == 0, odd, even), size, 1)

    share, table = low_rank_products(
        tok, tok_in, [*low, *stage0, *stage1, *stage2], grad_mine, grad_in, size,
        [r.array for r in sent],
    )
    hidden, names, terms = adapter_terms(
        share, swap(share, size, 1), tok, tok_in, grad_mine, grad_in, size, BF16
    )
    terms_sent = terms
    groups = [list(range(core, size, 2)) for core in range(2)]
    terms = lax.all_to_all(terms, "fsdp", 0, 0, axis_index_groups=groups, tiled=True)
    down_gradient, up_gradient = sum_terms(terms, names, size)

    early = [*wide[:3], *(r for stage in stages for r in stage)]
    shares = value_products(tok, tok_in, early, (), (hidden, table), size, ())
    wide[3].array = ordered(wide[3].array, terms_sent)
    for step in range(3, planes):
        _, stage = across([wide[step]], stages[-1], kinds, size)
        stages.append(stage)
    for rows in stages[-1]:
        rows.array = ordered(rows.array, shares[0])
    _, stage = across([], stages[-1], kinds, size)
    late = [*wide[3:], *(r for s in stages[4:] for r in s)]
    shares = value_products(tok, tok_in, late, shares, (), size, (down_gradient,))
    keep, give = value_products(tok, tok_in, stage, shares, (), size, ())
    total = (keep + swap(give, size, 1)).reshape(-1, BLOCK, width)
    value = jnp.where(valid, total, 0.0).astype(BF16)
    right = jnp.sum(jnp.where(goes_right, value, zero), axis=0)
    left = jnp.sum(jnp.where(goes_left, value, zero), axis=0)
    own = jnp.where(stays, value, zero)
    lower, upper = shift(right, size, 1), shift(left, size, -1)
    layer_out = jnp.concatenate([lower[None], own, upper[None]]).reshape(-1, width)
    return layer_out, down_gradient, up_gradient


def solution(mesh):
    rows = P(("groups", "fsdp"), None)
    vector = P(("groups", "fsdp"))
    in_specs = (rows, P("fsdp", None), rows, P("groups", "fsdp"), vector, vector, vector, rows)
    out_specs = (rows, rows, P("groups", "fsdp"))
    return jax.shard_map(
        functools.partial(body, mesh.shape["fsdp"]),
        mesh=mesh,
        in_specs=in_specs,
        out_specs=out_specs,
        check_vma=False,
    )
```

```python
import functools

import jax
import jax.numpy as jnp
from jax import lax
from jax.experimental import pallas as pl
from jax.experimental.pallas import tpu as pltpu
from jax.sharding import PartitionSpec as P

RANK = 16
COUNT = 16
BLOCK = 128
WIDE = RANK * COUNT
SCALE = 2.0
MIB = 1 << 20
F32 = jnp.float32
BF16 = jnp.bfloat16
VMEM = pl.BlockSpec(memory_space=pltpu.VMEM)
ANY = pl.BlockSpec(memory_space=pl.ANY)


def send_to(x, size, target):
    return lax.ppermute(x, "fsdp", [(i, target(i)) for i in range(size)])


def swap(x, size, bit):
    return send_to(x, size, lambda i: i ^ bit)


def turn(x, size, planes):
    return send_to(x, size, lambda i: (i + 8 * planes) % size)


def shift(x, size, step):
    pairs = [(i, i + step) for i in range(size) if 0 <= i + step < size]
    return lax.ppermute(x, "fsdp", pairs)


def chip_at(me, planes, group, step):
    chip = me // 2
    z = chip // 4
    y = (chip // 2) % 2
    x = chip % 2
    if group & 1:
        y = 1 - y
    if group & 2:
        x = 1 - x
    return lax.rem(z + planes - step, planes) * 4 + y * 2 + x


def ordered(x, *before):
    return lax.optimization_barrier((x, *before))[0]


class Rows:
    def __init__(self, array, parts):
        self.array = array
        self.parts = parts

    def part(self, kind, begin, count):
        parts, row, seen, first = [], 0, 0, None
        for k, group, step, at, n in self.parts:
            if k == kind and group in (1, 2):
                low, high = max(begin, seen), min(begin + count, seen + n)
                if low < high:
                    parts.append((k, group, step, at + low - seen, high - low))
                    first = row + low - seen if first is None else first
                seen += n
            row += n
        return first, count, parts

    def count(self, kind):
        return sum(n for k, group, _, _, n in self.parts if k == kind and group in (1, 2))

    def swapped(self, size, group):
        parts = [(k, g ^ group, s, at, n) for k, g, s, at, n in self.parts]
        return Rows(swap(self.array, size, 4 // group), parts)

    def turned(self, size, planes):
        parts = [(k, g, s + planes, at, n) for k, g, s, at, n in self.parts]
        return Rows(turn(self.array, size, planes), parts)


def packed(takes, sources):
    takes = [take for take in takes if take]
    counts = [sum(n for _, _, n in take) for take in takes]

    def kernel(*refs):
        for take, out in zip(takes, refs[len(sources) :]):
            row = 0
            for source, first, n in take:
                out[row : row + n] = refs[source][first : first + n]
                row += n

    return pl.pallas_call(
        kernel,
        out_shape=[jax.ShapeDtypeStruct((n, sources[0].shape[1]), BF16) for n in counts],
        in_specs=[VMEM] * len(sources),
        out_specs=[VMEM] * len(takes),
        compiler_params=pltpu.CompilerParams(vmem_limit_bytes=12 * MIB),
        cost_estimate=pl.CostEstimate(flops=0, bytes_accessed=4 * MIB, transcendentals=0),
        name="packed",
    )(*sources)


def across(line, previous, kinds, size):
    rows = [*line, *(previous or ())]
    takes, parts = ([], []), ([], [])
    for n, r in enumerate(line):
        for way in range(2):
            takes[way].append((n, 0, r.array.shape[0]))
            parts[way].extend(r.parts)
    if previous:
        for kind, unit in kinds:
            total = previous[0].count(kind)
            cut = total // 2 // unit * unit
            for way, begin, count in ((1, 0, cut), (0, cut, total - cut)):
                if count:
                    first, n, what = previous[1 - way].part(kind, begin, count)
                    takes[way].append((len(line) + 1 - way, first, n))
                    parts[way].extend(what)
    if previous:
        arrays = packed(takes, [r.array for r in rows])
    else:
        arrays = [jnp.concatenate([r.array for r in line])] * 2
    ways = [way for way in range(2) if takes[way]]
    sent = [Rows(array, parts[way]) for way, array in zip(ways, arrays)]
    return sent, [r.swapped(size, 1 + way) for way, r in zip(ways, sent)]


def split_tokens(tokens, size):
    rows, width = tokens.shape
    depth = width // size
    chips = size // 2
    planes = size // 8

    def kernel(tok, mine, other, far):
        me = lax.axis_index("fsdp")
        core = lax.rem(me, 2)
        for i in range(chips):
            chip = chip_at(me, planes, i // planes, i % planes)
            for ref, parity in ((other, 1 - core), (mine, core)):
                start = pl.multiple_of((2 * chip + parity) * depth, depth)
                ref[:, i * depth : (i + 1) * depth] = tok[:, pl.ds(start, depth)]
        far[...] = mine[:, chips * depth // 2 :]

    half = jax.ShapeDtypeStruct((rows, width // 2), tokens.dtype)
    return pl.pallas_call(
        kernel,
        out_shape=(half, half, jax.ShapeDtypeStruct((rows, width // 4), tokens.dtype)),
        in_specs=[VMEM],
        out_specs=(VMEM, VMEM, VMEM),
        compiler_params=pltpu.CompilerParams(vmem_limit_bytes=16 * MIB),
        cost_estimate=pl.CostEstimate(flops=0, bytes_accessed=4 * rows * width, transcendentals=0),
        name="split_tokens",
    )(tokens)


def dot(a, b):
    return jnp.dot(a, b, preferred_element_type=F32)


def dot_nt(a, b):
    return lax.dot_general(a, b, (((1,), (1,)), ((), ())), preferred_element_type=F32)


def dot_tn(a, b):
    return lax.dot_general(a, b, (((0,), (0,)), ((), ())), preferred_element_type=F32)


def low_rank_products(tok, tok_in, pieces, grad, grad_in, size, after):
    rows = tok.shape[0]
    depth = tok.shape[1] * 2 // size
    planes = size // 8
    deep = depth // 4
    quarters = 2 * depth // 256
    count = len(pieces)

    def kernel(tok, tok_in, *refs):
        refs, (grad, grad_in), (out, table, down) = refs[:count], refs[count : count + 2], refs[-3:]
        me = lax.axis_index("fsdp")
        meta = jnp.zeros((16, WIDE), F32)
        for ref, piece in zip(refs, pieces):
            row = 0
            for kind, group, step, at, n in piece.parts:
                begin, row = row, row + n
                if kind != "low":
                    continue
                spot = group * planes + step
                n_down = min(n, deep - at)
                if n_down > 0:
                    for g in range(4):
                        to = spot * depth + g * deep + at
                        down[to : to + n_down] = ref[begin : begin + n_down, g * 256 : (g + 1) * 256]
                if at + n <= deep:
                    continue
                last = slice(row - 16, row)
                chip = chip_at(me, planes, group, step)
                for q in range(quarters):
                    flat = chip * quarters + q
                    to = pl.multiple_of(flat // 2 * RANK, RANK)
                    table[lax.rem(flat, 2), pl.ds(to, RANK), :] = ref[last, q * 256 : (q + 1) * 256]
                meta += ref[last, 512 : 512 + WIDE].astype(F32)
        for half, source in enumerate((tok, tok_in)):
            out[half * rows : (half + 1) * rows] = dot(source[...], down[...])
        for half, source in enumerate((grad, grad_in)):
            low = dot_nt(source[:, :256], table[0]) + dot_nt(source[:, 256:], table[1])
            out[(2 + half) * rows : (3 + half) * rows] = low
        out[4 * rows :] = meta

    return pl.pallas_call(
        kernel,
        out_shape=(
            jax.ShapeDtypeStruct((4 * rows + 16, WIDE), F32),
            jax.ShapeDtypeStruct((2, WIDE, 256), BF16),
        ),
        in_specs=[VMEM] * (4 + count) + [ANY] * len(after),
        out_specs=(VMEM, VMEM),
        scratch_shapes=[pltpu.VMEM((tok.shape[1], WIDE), BF16)],
        compiler_params=pltpu.CompilerParams(vmem_limit_bytes=24 * MIB),
        cost_estimate=pl.CostEstimate(
            flops=4 * rows * (tok.shape[1] + 512) * WIDE, bytes_accessed=9 * MIB, transcendentals=0
        ),
        name="low_rank_products",
    )(tok, tok_in, *(p.array for p in pieces), grad, grad_in, *after)


def adapter_terms(own, other, tok, tok_in, grad, grad_in, size, kind, after):
    rows = tok.shape[0]
    depth = tok.shape[1] * 2 // size
    planes = size // 8
    slices = 512 // depth

    def kernel(own, other, tok, tok_in, grad, grad_in, *refs):
        hidden, names, terms = refs[-3:]
        me = lax.axis_index("fsdp")
        table = own[4 * rows :] + other[4 * rows :]
        names[...] = table
        lane = lax.broadcasted_iota(jnp.int32, (1, WIDE), 1)
        row = lax.broadcasted_iota(jnp.int32, (rows, 1), 0)
        adapter_of_lane = (lane // RANK).astype(F32)
        fold_row = lax.broadcasted_iota(jnp.int32, (WIDE, 2 * RANK), 0)
        fold_lane = lax.broadcasted_iota(jnp.int32, (WIDE, 2 * RANK), 1)
        fold = (fold_row % RANK == fold_lane % RANK).astype(F32).astype(BF16)
        block_lane = lax.broadcasted_iota(jnp.int32, (rows, 2 * RANK), 1) // RANK
        block_row = lax.broadcasted_iota(jnp.int32, (rows, 2 * RANK), 0) // BLOCK
        for half, source in enumerate((tok, tok_in)):
            device = me if half == 0 else me + 1 - 2 * lax.rem(me, 2)
            found = [
                jnp.sum(jnp.where(lane == device, table[b : b + 1], 0.0), axis=1, keepdims=True)
                for b in range(2)
            ]
            adapter = jnp.where(row < BLOCK, found[0], found[1])
            chosen = adapter_of_lane == adapter
            mine, theirs = half * rows, (1 - half) * rows
            act = own[mine : mine + rows] + other[theirs : theirs + rows]
            hidden[mine : mine + rows] = jnp.where(chosen, act, 0.0).astype(BF16)
            mine, theirs = mine + 2 * rows, theirs + 2 * rows
            low = own[mine : mine + rows] + other[theirs : theirs + rows]
            low = jnp.where(chosen, low, 0.0).astype(BF16)
            narrow = jnp.where(block_lane == block_row, dot(low, fold), 0.0).astype(BF16)
            for i in range(4 * planes):
                chip = chip_at(me, planes, i // planes, i % planes)
                term = dot_tn(narrow, source[:, i * depth : (i + 1) * depth])
                terms[chip, half * 32 : (half + 1) * 32, :] = term.astype(kind)
        up = dot_tn(hidden[:rows], grad[...]) + dot_tn(hidden[rows:], grad_in[...])
        for a in range(COUNT):
            for t in range(slices):
                chip, place = divmod(a * slices + t, 2)
                terms[chip, 64 + 16 * place : 80 + 16 * place, :] = up[
                    a * RANK : (a + 1) * RANK, t * depth : (t + 1) * depth
                ].astype(kind)

    return pl.pallas_call(
        kernel,
        out_shape=(
            jax.ShapeDtypeStruct((2 * rows, WIDE), BF16),
            jax.ShapeDtypeStruct((16, WIDE), F32),
            jax.ShapeDtypeStruct((size // 2, 96, depth), kind),
        ),
        in_specs=[VMEM] * 6 + [ANY] * len(after),
        out_specs=(VMEM, VMEM, VMEM),
        compiler_params=pltpu.CompilerParams(vmem_limit_bytes=24 * MIB),
        cost_estimate=pl.CostEstimate(
            flops=4 * rows * tok.shape[1] * 128, bytes_accessed=9 * MIB, transcendentals=0
        ),
        name="adapter_terms",
    )(own, other, tok, tok_in, grad, grad_in, *after)


def sum_terms(terms, names, size):
    chips, _, depth = terms.shape

    def kernel(terms, names, down, up):
        core = lax.rem(lax.axis_index("fsdp"), 2)
        count = chips * 64
        device = lax.broadcasted_iota(jnp.int32, (WIDE, count), 0)
        spot = lax.broadcasted_iota(jnp.int32, (WIDE, count), 1)
        block = (spot // 16) % 4
        sender = 2 * (spot // 64) + jnp.where(block < 2, core, 1 - core)
        table = names[...].astype(BF16)
        first = ((device == sender) & (block % 2 == 0)).astype(F32).astype(BF16)
        second = ((device == sender) & (block % 2 == 1)).astype(F32).astype(BF16)
        adapter = (dot(table, first)[0:1] + dot(table, second)[1:2]).astype(jnp.int32)
        pick = (device == adapter * RANK + spot % RANK).astype(F32)
        source = terms[:, :64, :].reshape(count, depth)
        if terms.dtype == BF16:
            total = dot(pick.astype(BF16), source)
        else:
            total = jnp.dot(
                pick, source, preferred_element_type=F32, precision=lax.Precision.HIGHEST
            )
        down[...] = SCALE * total.T
        for s in range(2):
            up[:, s * depth : (s + 1) * depth] = SCALE * jnp.sum(
                terms[:, 64 + 16 * s : 80 + 16 * s, :].astype(F32), axis=0
            )

    return pl.pallas_call(
        kernel,
        out_shape=(
            jax.ShapeDtypeStruct((depth, WIDE), F32),
            jax.ShapeDtypeStruct((RANK, 2 * depth), F32),
        ),
        in_specs=[VMEM] * 2,
        out_specs=(VMEM, VMEM),
        compiler_params=pltpu.CompilerParams(vmem_limit_bytes=24 * MIB),
        cost_estimate=pl.CostEstimate(
            flops=2 * WIDE * chips * 64 * depth, bytes_accessed=2 * MIB, transcendentals=0
        ),
        name="sum_terms",
    )(terms, names)


def value_products(tok, tok_in, tok_far, pieces, so_far, adapters, size, after):
    rows = tok.shape[0]
    depth = tok.shape[1] * 2 // size
    planes = size // 8
    own_columns = 2 * depth
    width = pieces[0].array.shape[1]
    count = len(pieces)
    terms = []
    for n, piece in enumerate(pieces):
        row = 0
        for kind, group, step, at, height in piece.parts:
            terms.append((n, row, (group * planes + step) * depth + at, height))
            row += height
    joint = (*so_far, *adapters)
    n_joint = len(joint)

    def kernel(tok, tok_in, far, far_in, *refs):
        refs, joint, (keep, give) = refs[:count], refs[count : count + n_joint], refs[-2:]
        core = lax.rem(lax.axis_index("fsdp"), 2)
        for chip in range(2):
            for half, out in enumerate((keep, give)):
                to = slice(chip * rows, (chip + 1) * rows)
                for left in range(0, width, 256):
                    here = slice(left, left + 256)
                    total = joint[half][to, here] if so_far else jnp.zeros((rows, 256), F32)
                    if adapters and not chip:
                        hidden, table = joint[-2:]
                        owner = left // own_columns
                        place = (owner // 2 * own_columns + left % own_columns) // 256
                        scale = jnp.where(core == owner % 2, SCALE, 0.0).astype(F32)
                        total += scale * dot(hidden[half * rows : (half + 1) * rows], table[place])
                    for n, row, spot, height in terms:
                        columns = slice(spot, spot + height)
                        if chip:
                            left_side = (far, far_in)[half][:, columns]
                        else:
                            left_side = (tok, tok_in)[half][:, columns]
                        total += dot(left_side, refs[n][row : row + height, here])
                    out[to, here] = total

    share = jax.ShapeDtypeStruct((2 * rows, width), F32)
    return pl.pallas_call(
        kernel,
        out_shape=(share, share),
        in_specs=[VMEM] * (4 + count + n_joint) + [ANY] * len(after),
        out_specs=(VMEM, VMEM),
        compiler_params=pltpu.CompilerParams(vmem_limit_bytes=40 * MIB),
        cost_estimate=pl.CostEstimate(
            flops=8 * rows * sum(t[3] for t in terms) * width,
            bytes_accessed=4 * MIB,
            transcendentals=0,
        ),
        name="value_products",
    )(tok, tok_in, *tok_far, *(p.array for p in pieces), *joint, *after)


def body(
    size,
    tokens,
    frozen_value_weight,
    adapter_down_weight,
    adapter_up_weight,
    block_adapter_index,
    block_valid_length,
    destinations,
    cotangent,
):
    width = frozen_value_weight.shape[1]
    own_columns = adapter_up_weight.shape[1]
    me = lax.axis_index("fsdp")
    core = me % 2
    goes_right = (destinations == me + 1)[:, None, None]
    goes_left = (destinations == me - 1)[:, None, None]
    stays = (destinations == me)[:, None, None]
    valid = (jnp.arange(BLOCK)[None, :] < block_valid_length[:, None])[..., None]
    zero = jnp.zeros((), BF16)

    depth = adapter_down_weight.shape[0]
    deep = depth // 4
    planes = size // 8
    lane = jnp.arange(WIDE)[None, :]
    meta = jnp.where(lane == me, block_adapter_index[:, None], 0).astype(BF16)
    meta = jnp.pad(meta, ((0, 14), (0, 0)))
    downs = [adapter_down_weight[g * deep : (g + 1) * deep] for g in range(4)]
    ups = jnp.pad(adapter_up_weight, ((0, 0), (0, 512 - own_columns)))
    last_rows = jnp.concatenate([ups, meta, jnp.zeros_like(meta)], axis=1)
    low_piece = jnp.concatenate([jnp.concatenate(downs, axis=1), last_rows])
    low = [Rows(low_piece, [("low", 0, 0, 0, deep + 16)])]
    wide = [Rows(frozen_value_weight, [("wide", 0, 0, 0, depth)])]
    kinds = (("low", 16),)

    low += [low[0].turned(size, step) for step in range(1, planes)]
    wide[0].array = ordered(wide[0].array, *(r.array for r in low[1:]))
    for step in range(planes - 1):
        wide.append(wide[-1].turned(size, 1))
    wide[0].array = frozen_value_weight
    wide_y = [r.swapped(size, 1) for r in wide]
    _, stage0 = across(low[:1], None, kinds, size)
    wide_y[0] = Rows(ordered(frozen_value_weight, *(r.array for r in stage0)), wide[0].parts).swapped(size, 1)

    tok, tok_out, far_out = split_tokens(tokens, size)
    far_own = swap(far_out, size, 2)
    tok_in = swap(tok_out, size, 1)
    near = tok.shape[1] // 2

    slots = cotangent.reshape(-1, BLOCK, width)
    from_upper = shift(slots[0], size, -1)
    from_lower = shift(slots[-1], size, 1)
    grad = jnp.where(goes_right, from_upper[None], jnp.where(goes_left, from_lower[None], slots[1:-1]))
    grad = jnp.where(valid, grad, zero).reshape(-1, width)
    runs = [grad[:, i : i + own_columns] for i in range(0, width, own_columns)]
    even, odd = jnp.concatenate(runs[0::2], axis=1), jnp.concatenate(runs[1::2], axis=1)
    grad_mine = jnp.where(core == 0, even, odd)
    grad_in = swap(jnp.where(core == 0, odd, even), size, 1)

    _, stage1 = across(low[1:], stage0, kinds, size)
    _, stage2 = across([], stage1, kinds, size)
    far_columns = ordered(tok_in[:, near:], *(r.array for r in stage1))
    tok_far = (far_own, swap(far_columns, size, 2))
    share, table = low_rank_products(
        tok, tok_in, [*low, *stage0, *stage1, *stage2], grad_mine, grad_in, size,
        (wide[1].array, far_columns, ),
    )
    hidden, names, terms = adapter_terms(
        share, swap(share, size, 1), tok, tok_in, grad_mine, grad_in, size, BF16, ()
    )
    terms_sent = terms
    groups = [list(range(core, size, 2)) for core in range(2)]
    terms = lax.all_to_all(terms, "fsdp", 0, 0, axis_index_groups=groups, tiled=True)
    down_gradient, up_gradient = sum_terms(terms, names, size)

    early = [*wide, *wide_y[:-2]]
    late = wide_y[-2:]
    shares = value_products(tok, tok_in, tok_far, early, (), (), size, ())
    keep, give = value_products(
        tok, tok_in, tok_far, late, shares, (hidden, table), size, ()
    )
    both = keep + swap(give, size, 1)
    rows = both.shape[0] // 2
    far = swap(both[rows:].astype(BF16), size, 2)
    total = (both[:rows] + far.astype(F32)).reshape(-1, BLOCK, width)
    value = jnp.where(valid, total, 0.0).astype(BF16)
    right = jnp.sum(jnp.where(goes_right, value, zero), axis=0)
    left = jnp.sum(jnp.where(goes_left, value, zero), axis=0)
    own = jnp.where(stays, value, zero)
    lower, upper = shift(right, size, 1), shift(left, size, -1)
    own = ordered(own, down_gradient)
    layer_out = jnp.concatenate([lower[None], own, upper[None]]).reshape(-1, width)
    return layer_out, down_gradient, up_gradient


def solution(mesh):
    rows = P(("groups", "fsdp"), None)
    vector = P(("groups", "fsdp"))
    in_specs = (rows, P("fsdp", None), rows, P("groups", "fsdp"), vector, vector, vector, rows)
    out_specs = (rows, rows, P("groups", "fsdp"))
    return jax.shard_map(
        functools.partial(body, mesh.shape["fsdp"]),
        mesh=mesh,
        in_specs=in_specs,
        out_specs=out_specs,
        check_vma=False,
    )
```

```python
import functools

import jax
import jax.numpy as jnp
from jax import lax
from jax.experimental import pallas as pl
from jax.experimental.pallas import tpu as pltpu
from jax.sharding import PartitionSpec as P

RANK = 16
COUNT = 16
BLOCK = 128
WIDE = RANK * COUNT
SCALE = 2.0
MIB = 1 << 20
F32 = jnp.float32
BF16 = jnp.bfloat16
VMEM = pl.BlockSpec(memory_space=pltpu.VMEM)
ANY = pl.BlockSpec(memory_space=pl.ANY)


def send_to(x, size, target):
    return lax.ppermute(x, "fsdp", [(i, target(i)) for i in range(size)])


def swap(x, size, bit):
    return send_to(x, size, lambda i: i ^ bit)


def turn(x, size, planes):
    return send_to(x, size, lambda i: (i + 8 * planes) % size)


def shift(x, size, step):
    pairs = [(i, i + step) for i in range(size) if 0 <= i + step < size]
    return lax.ppermute(x, "fsdp", pairs)


def chip_at(me, planes, group, step):
    chip = me // 2
    z = chip // 4
    y = (chip // 2) % 2
    x = chip % 2
    if group & 1:
        y = 1 - y
    if group & 2:
        x = 1 - x
    return lax.rem(z + planes - step, planes) * 4 + y * 2 + x


def ordered(x, *before):
    return lax.optimization_barrier((x, *before))[0]


class Rows:
    def __init__(self, array, parts):
        self.array = array
        self.parts = parts

    def part(self, kind, begin, count):
        parts, row, seen, first = [], 0, 0, None
        for k, group, step, at, n in self.parts:
            if k == kind and group in (1, 2):
                low, high = max(begin, seen), min(begin + count, seen + n)
                if low < high:
                    parts.append((k, group, step, at + low - seen, high - low))
                    first = row + low - seen if first is None else first
                seen += n
            row += n
        return first, count, parts

    def count(self, kind):
        return sum(n for k, group, _, _, n in self.parts if k == kind and group in (1, 2))

    def swapped(self, size, group):
        parts = [(k, g ^ group, s, at, n) for k, g, s, at, n in self.parts]
        return Rows(swap(self.array, size, 4 // group), parts)

    def turned(self, size, planes):
        parts = [(k, g, s + planes, at, n) for k, g, s, at, n in self.parts]
        return Rows(turn(self.array, size, planes), parts)


def packed(takes, sources):
    takes = [take for take in takes if take]
    counts = [sum(n for _, _, n in take) for take in takes]

    def kernel(*refs):
        for take, out in zip(takes, refs[len(sources) :]):
            row = 0
            for source, first, n in take:
                out[row : row + n] = refs[source][first : first + n]
                row += n

    return pl.pallas_call(
        kernel,
        out_shape=[jax.ShapeDtypeStruct((n, sources[0].shape[1]), BF16) for n in counts],
        in_specs=[VMEM] * len(sources),
        out_specs=[VMEM] * len(takes),
        compiler_params=pltpu.CompilerParams(vmem_limit_bytes=12 * MIB),
        cost_estimate=pl.CostEstimate(flops=0, bytes_accessed=4 * MIB, transcendentals=0),
        name="packed",
    )(*sources)


def across(line, previous, kinds, size):
    rows = [*line, *(previous or ())]
    takes, parts = ([], []), ([], [])
    for n, r in enumerate(line):
        for way in range(2):
            takes[way].append((n, 0, r.array.shape[0]))
            parts[way].extend(r.parts)
    if previous:
        for kind, unit in kinds:
            total = previous[0].count(kind)
            cut = total // 2 // unit * unit
            for way, begin, count in ((1, 0, cut), (0, cut, total - cut)):
                if count:
                    first, n, what = previous[1 - way].part(kind, begin, count)
                    takes[way].append((len(line) + 1 - way, first, n))
                    parts[way].extend(what)
    if previous:
        arrays = packed(takes, [r.array for r in rows])
    else:
        arrays = [jnp.concatenate([r.array for r in line])] * 2
    ways = [way for way in range(2) if takes[way]]
    sent = [Rows(array, parts[way]) for way, array in zip(ways, arrays)]
    return sent, [r.swapped(size, 1 + way) for way, r in zip(ways, sent)]


def split_tokens(tokens, size):
    rows, width = tokens.shape
    depth = width // size
    chips = size // 2
    planes = size // 8

    def kernel(tok, mine, other, far):
        me = lax.axis_index("fsdp")
        core = lax.rem(me, 2)
        for i in range(chips):
            chip = chip_at(me, planes, i // planes, i % planes)
            for ref, parity in ((other, 1 - core), (mine, core)):
                start = pl.multiple_of((2 * chip + parity) * depth, depth)
                ref[:, i * depth : (i + 1) * depth] = tok[:, pl.ds(start, depth)]
        far[...] = mine[:, chips * depth // 2 :]

    half = jax.ShapeDtypeStruct((rows, width // 2), tokens.dtype)
    return pl.pallas_call(
        kernel,
        out_shape=(half, half, jax.ShapeDtypeStruct((rows, width // 4), tokens.dtype)),
        in_specs=[VMEM],
        out_specs=(VMEM, VMEM, VMEM),
        compiler_params=pltpu.CompilerParams(vmem_limit_bytes=16 * MIB),
        cost_estimate=pl.CostEstimate(flops=0, bytes_accessed=4 * rows * width, transcendentals=0),
        name="split_tokens",
    )(tokens)


def dot(a, b):
    return jnp.dot(a, b, preferred_element_type=F32)


def dot_nt(a, b):
    return lax.dot_general(a, b, (((1,), (1,)), ((), ())), preferred_element_type=F32)


def dot_tn(a, b):
    return lax.dot_general(a, b, (((0,), (0,)), ((), ())), preferred_element_type=F32)


def low_rank_products(tok, tok_in, pieces, grad, grad_in, size, after):
    rows = tok.shape[0]
    depth = tok.shape[1] * 2 // size
    planes = size // 8
    deep = depth // 4
    quarters = 2 * depth // 256
    count = len(pieces)

    def kernel(tok, tok_in, *refs):
        refs, (grad, grad_in), (out, table, down) = refs[:count], refs[count : count + 2], refs[-3:]
        me = lax.axis_index("fsdp")
        meta = jnp.zeros((16, WIDE), F32)
        for ref, piece in zip(refs, pieces):
            row = 0
            for kind, group, step, at, n in piece.parts:
                begin, row = row, row + n
                if kind != "low":
                    continue
                spot = group * planes + step
                n_down = min(n, deep - at)
                if n_down > 0:
                    for g in range(4):
                        to = spot * depth + g * deep + at
                        down[to : to + n_down] = ref[begin : begin + n_down, g * 256 : (g + 1) * 256]
                if at + n <= deep:
                    continue
                last = slice(row - 16, row)
                chip = chip_at(me, planes, group, step)
                for q in range(quarters):
                    flat = chip * quarters + q
                    to = pl.multiple_of(flat // 2 * RANK, RANK)
                    table[lax.rem(flat, 2), pl.ds(to, RANK), :] = ref[last, q * 256 : (q + 1) * 256]
                meta += ref[last, 512 : 512 + WIDE].astype(F32)
        for half, source in enumerate((tok, tok_in)):
            out[half * rows : (half + 1) * rows] = dot(source[...], down[...])
        for half, source in enumerate((grad, grad_in)):
            low = dot_nt(source[:, :256], table[0]) + dot_nt(source[:, 256:], table[1])
            out[(2 + half) * rows : (3 + half) * rows] = low
        out[4 * rows :] = meta

    return pl.pallas_call(
        kernel,
        out_shape=(
            jax.ShapeDtypeStruct((4 * rows + 16, WIDE), F32),
            jax.ShapeDtypeStruct((2, WIDE, 256), BF16),
        ),
        in_specs=[VMEM] * (4 + count) + [ANY] * len(after),
        out_specs=(VMEM, VMEM),
        scratch_shapes=[pltpu.VMEM((tok.shape[1], WIDE), BF16)],
        compiler_params=pltpu.CompilerParams(vmem_limit_bytes=24 * MIB),
        cost_estimate=pl.CostEstimate(
            flops=4 * rows * (tok.shape[1] + 512) * WIDE, bytes_accessed=9 * MIB, transcendentals=0
        ),
        name="low_rank_products",
    )(tok, tok_in, *(p.array for p in pieces), grad, grad_in, *after)


def adapter_terms(own, other, tok, tok_in, grad, grad_in, size, kind, after):
    rows = tok.shape[0]
    depth = tok.shape[1] * 2 // size
    planes = size // 8
    slices = 512 // depth

    def kernel(own, other, tok, tok_in, grad, grad_in, *refs):
        hidden, names, terms = refs[-3:]
        me = lax.axis_index("fsdp")
        table = own[4 * rows :] + other[4 * rows :]
        names[...] = table
        lane = lax.broadcasted_iota(jnp.int32, (1, WIDE), 1)
        row = lax.broadcasted_iota(jnp.int32, (rows, 1), 0)
        adapter_of_lane = (lane // RANK).astype(F32)
        fold_row = lax.broadcasted_iota(jnp.int32, (WIDE, 2 * RANK), 0)
        fold_lane = lax.broadcasted_iota(jnp.int32, (WIDE, 2 * RANK), 1)
        fold = (fold_row % RANK == fold_lane % RANK).astype(F32).astype(BF16)
        block_lane = lax.broadcasted_iota(jnp.int32, (rows, 2 * RANK), 1) // RANK
        block_row = lax.broadcasted_iota(jnp.int32, (rows, 2 * RANK), 0) // BLOCK
        for half, source in enumerate((tok, tok_in)):
            device = me if half == 0 else me + 1 - 2 * lax.rem(me, 2)
            found = [
                jnp.sum(jnp.where(lane == device, table[b : b + 1], 0.0), axis=1, keepdims=True)
                for b in range(2)
            ]
            adapter = jnp.where(row < BLOCK, found[0], found[1])
            chosen = adapter_of_lane == adapter
            mine, theirs = half * rows, (1 - half) * rows
            act = own[mine : mine + rows] + other[theirs : theirs + rows]
            hidden[mine : mine + rows] = jnp.where(chosen, act, 0.0).astype(BF16)
            mine, theirs = mine + 2 * rows, theirs + 2 * rows
            low = own[mine : mine + rows] + other[theirs : theirs + rows]
            low = jnp.where(chosen, low, 0.0).astype(BF16)
            narrow = jnp.where(block_lane == block_row, dot(low, fold), 0.0).astype(BF16)
            for i in range(4 * planes):
                chip = chip_at(me, planes, i // planes, i % planes)
                term = dot_tn(narrow, source[:, i * depth : (i + 1) * depth])
                terms[chip, half * 32 : (half + 1) * 32, :] = term.astype(kind)
        up = dot_tn(hidden[:rows], grad[...]) + dot_tn(hidden[rows:], grad_in[...])
        for a in range(COUNT):
            for t in range(slices):
                chip, place = divmod(a * slices + t, 2)
                terms[chip, 64 + 16 * place : 80 + 16 * place, :] = up[
                    a * RANK : (a + 1) * RANK, t * depth : (t + 1) * depth
                ].astype(kind)

    return pl.pallas_call(
        kernel,
        out_shape=(
            jax.ShapeDtypeStruct((2 * rows, WIDE), BF16),
            jax.ShapeDtypeStruct((16, WIDE), F32),
            jax.ShapeDtypeStruct((size // 2, 96, depth), kind),
        ),
        in_specs=[VMEM] * 6 + [ANY] * len(after),
        out_specs=(VMEM, VMEM, VMEM),
        compiler_params=pltpu.CompilerParams(vmem_limit_bytes=24 * MIB),
        cost_estimate=pl.CostEstimate(
            flops=4 * rows * tok.shape[1] * 128, bytes_accessed=9 * MIB, transcendentals=0
        ),
        name="adapter_terms",
    )(own, other, tok, tok_in, grad, grad_in, *after)


def sum_terms(terms, names, size):
    chips, _, depth = terms.shape

    def kernel(terms, names, down, up):
        core = lax.rem(lax.axis_index("fsdp"), 2)
        count = chips * 64
        device = lax.broadcasted_iota(jnp.int32, (WIDE, count), 0)
        spot = lax.broadcasted_iota(jnp.int32, (WIDE, count), 1)
        block = (spot // 16) % 4
        sender = 2 * (spot // 64) + jnp.where(block < 2, core, 1 - core)
        table = names[...].astype(BF16)
        first = ((device == sender) & (block % 2 == 0)).astype(F32).astype(BF16)
        second = ((device == sender) & (block % 2 == 1)).astype(F32).astype(BF16)
        adapter = (dot(table, first)[0:1] + dot(table, second)[1:2]).astype(jnp.int32)
        pick = (device == adapter * RANK + spot % RANK).astype(F32)
        source = terms[:, :64, :].reshape(count, depth)
        if terms.dtype == BF16:
            total = dot(pick.astype(BF16), source)
        else:
            total = jnp.dot(
                pick, source, preferred_element_type=F32, precision=lax.Precision.HIGHEST
            )
        down[...] = SCALE * total.T
        for s in range(2):
            up[:, s * depth : (s + 1) * depth] = SCALE * jnp.sum(
                terms[:, 64 + 16 * s : 80 + 16 * s, :].astype(F32), axis=0
            )

    return pl.pallas_call(
        kernel,
        out_shape=(
            jax.ShapeDtypeStruct((depth, WIDE), F32),
            jax.ShapeDtypeStruct((RANK, 2 * depth), F32),
        ),
        in_specs=[VMEM] * 2,
        out_specs=(VMEM, VMEM),
        compiler_params=pltpu.CompilerParams(vmem_limit_bytes=24 * MIB),
        cost_estimate=pl.CostEstimate(
            flops=2 * WIDE * chips * 64 * depth, bytes_accessed=2 * MIB, transcendentals=0
        ),
        name="sum_terms",
    )(terms, names)


def value_products(tok, tok_in, tok_far, pieces, so_far, adapters, size, after):
    rows = tok.shape[0]
    depth = tok.shape[1] * 2 // size
    planes = size // 8
    own_columns = 2 * depth
    width = pieces[0].array.shape[1]
    count = len(pieces)
    terms = []
    for n, piece in enumerate(pieces):
        row = 0
        for kind, group, step, at, height in piece.parts:
            terms.append((n, row, (group * planes + step) * depth + at, height))
            row += height
    joint = (*so_far, *adapters)
    n_joint = len(joint)

    def kernel(tok, tok_in, far, far_in, *refs):
        refs, joint, (keep, give) = refs[:count], refs[count : count + n_joint], refs[-2:]
        core = lax.rem(lax.axis_index("fsdp"), 2)
        for chip in range(2):
            for half, out in enumerate((keep, give)):
                to = slice(chip * rows, (chip + 1) * rows)
                for left in range(0, width, 256):
                    here = slice(left, left + 256)
                    total = joint[half][to, here] if so_far else jnp.zeros((rows, 256), F32)
                    if adapters and not chip:
                        hidden, table = joint[-2:]
                        owner = left // own_columns
                        place = (owner // 2 * own_columns + left % own_columns) // 256
                        scale = jnp.where(core == owner % 2, SCALE, 0.0).astype(F32)
                        total += scale * dot(hidden[half * rows : (half + 1) * rows], table[place])
                    for n, row, spot, height in terms:
                        columns = slice(spot, spot + height)
                        if chip:
                            left_side = (far, far_in)[half][:, columns]
                        else:
                            left_side = (tok, tok_in)[half][:, columns]
                        total += dot(left_side, refs[n][row : row + height, here])
                    out[to, here] = total.astype(out.dtype)

    share = jax.ShapeDtypeStruct((2 * rows, width), F32)
    return pl.pallas_call(
        kernel,
        out_shape=(share, jax.ShapeDtypeStruct(share.shape, BF16) if adapters else share),
        in_specs=[VMEM] * (4 + count + n_joint) + [ANY] * len(after),
        out_specs=(VMEM, VMEM),
        compiler_params=pltpu.CompilerParams(vmem_limit_bytes=40 * MIB),
        cost_estimate=pl.CostEstimate(
            flops=8 * rows * sum(t[3] for t in terms) * width,
            bytes_accessed=4 * MIB,
            transcendentals=0,
        ),
        name="value_products",
    )(tok, tok_in, *tok_far, *(p.array for p in pieces), *joint, *after)


def body(
    size,
    tokens,
    frozen_value_weight,
    adapter_down_weight,
    adapter_up_weight,
    block_adapter_index,
    block_valid_length,
    destinations,
    cotangent,
):
    width = frozen_value_weight.shape[1]
    own_columns = adapter_up_weight.shape[1]
    me = lax.axis_index("fsdp")
    core = me % 2
    goes_right = (destinations == me + 1)[:, None, None]
    goes_left = (destinations == me - 1)[:, None, None]
    stays = (destinations == me)[:, None, None]
    valid = (jnp.arange(BLOCK)[None, :] < block_valid_length[:, None])[..., None]
    zero = jnp.zeros((), BF16)

    depth = adapter_down_weight.shape[0]
    deep = depth // 4
    planes = size // 8
    lane = jnp.arange(WIDE)[None, :]
    meta = jnp.where(lane == me, block_adapter_index[:, None], 0).astype(BF16)
    meta = jnp.pad(meta, ((0, 14), (0, 0)))
    downs = [adapter_down_weight[g * deep : (g + 1) * deep] for g in range(4)]
    ups = jnp.pad(adapter_up_weight, ((0, 0), (0, 512 - own_columns)))
    last_rows = jnp.concatenate([ups, meta, jnp.zeros_like(meta)], axis=1)
    low_piece = jnp.concatenate([jnp.concatenate(downs, axis=1), last_rows])
    low = [Rows(low_piece, [("low", 0, 0, 0, deep + 16)])]
    wide = [Rows(frozen_value_weight, [("wide", 0, 0, 0, depth)])]
    kinds = (("low", 16),)

    low += [low[0].turned(size, step) for step in range(1, planes)]
    wide[0].array = ordered(wide[0].array, *(r.array for r in low[1:]))
    for step in range(planes - 1):
        wide.append(wide[-1].turned(size, 1))
    wide[0].array = frozen_value_weight
    wide_y = [r.swapped(size, 1) for r in wide]
    _, stage0 = across(low[:1], None, kinds, size)
    wide_y[0] = Rows(ordered(frozen_value_weight, *(r.array for r in stage0)), wide[0].parts).swapped(size, 1)

    tok, tok_out, far_out = split_tokens(tokens, size)
    far_own = swap(far_out, size, 2)
    tok_in = swap(tok_out, size, 1)
    near = tok.shape[1] // 2

    slots = cotangent.reshape(-1, BLOCK, width)
    from_upper = shift(slots[0], size, -1)
    from_lower = shift(slots[-1], size, 1)
    grad = jnp.where(goes_right, from_upper[None], jnp.where(goes_left, from_lower[None], slots[1:-1]))
    grad = jnp.where(valid, grad, zero).reshape(-1, width)
    runs = [grad[:, i : i + own_columns] for i in range(0, width, own_columns)]
    even, odd = jnp.concatenate(runs[0::2], axis=1), jnp.concatenate(runs[1::2], axis=1)
    grad_mine = jnp.where(core == 0, even, odd)
    grad_in = swap(jnp.where(core == 0, odd, even), size, 1)

    _, stage1 = across(low[1:], stage0, kinds, size)
    _, stage2 = across([], stage1, kinds, size)
    far_columns = ordered(tok_in[:, near:], *(r.array for r in stage1))
    tok_far = (far_own, swap(far_columns, size, 2))
    share, table = low_rank_products(
        tok, tok_in, [*low, *stage0, *stage1, *stage2], grad_mine, grad_in, size,
        (far_columns, ),
    )
    hidden, names, terms = adapter_terms(
        share, swap(share, size, 1), tok, tok_in, grad_mine, grad_in, size, BF16, (wide[2].array, )
    )
    terms_sent = terms
    groups = [list(range(core, size, 2)) for core in range(2)]
    terms = lax.all_to_all(terms, "fsdp", 0, 0, axis_index_groups=groups, tiled=True)
    down_gradient, up_gradient = sum_terms(terms, names, size)

    early = [*wide, *wide_y[:-2]]
    late = wide_y[-2:]
    shares = value_products(tok, tok_in, tok_far, early, (), (), size, ())
    keep, give = value_products(
        tok, tok_in, tok_far, late, shares, (hidden, table), size, ()
    )
    both = keep + swap(give, size, 1).astype(F32)
    rows = both.shape[0] // 2
    far = swap(both[rows:].astype(BF16), size, 2)
    total = (both[:rows] + far.astype(F32)).reshape(-1, BLOCK, width)
    value = jnp.where(valid, total, 0.0).astype(BF16)
    right = jnp.sum(jnp.where(goes_right, value, zero), axis=0)
    left = jnp.sum(jnp.where(goes_left, value, zero), axis=0)
    own = jnp.where(stays, value, zero)
    lower, upper = shift(right, size, 1), shift(left, size, -1)
    own = ordered(own, down_gradient)
    layer_out = jnp.concatenate([lower[None], own, upper[None]]).reshape(-1, width)
    return layer_out, down_gradient, up_gradient


def solution(mesh):
    rows = P(("groups", "fsdp"), None)
    vector = P(("groups", "fsdp"))
    in_specs = (rows, P("fsdp", None), rows, P("groups", "fsdp"), vector, vector, vector, rows)
    out_specs = (rows, rows, P("groups", "fsdp"))
    return jax.shard_map(
        functools.partial(body, mesh.shape["fsdp"]),
        mesh=mesh,
        in_specs=in_specs,
        out_specs=out_specs,
        check_vma=False,
    )
```
